32 devices in a mesh: groups: 2 (over y), row: 4 (over z), col: 2 (over x), freq: 2 (over core).
Axes of the slice: x: 2, y: 2, z: 4, core: 2. Of those that a mesh axis runs over, the one named last changes fastest.
Arguments:
- records: bfloat16 [16, 3072, 5120], P(('groups', 'freq'), ('row', 'col')), parts along dimension 0, may hold values from -1000 to 1000
- live_mask: int32 [10240], P(('groups', 'col')), parts along dimension 0, may hold values 0 or 1
- bin_index: int32 [8], P('groups'), parts along dimension 0, may hold values from 7 to 613
- block_order: int32 [8], P('groups'), parts along dimension 0, may hold values from 0 to 3, each once
Outputs:
- cross_stack: float32 [8, 2, 5120, 5120], P(('groups', 'freq'), None, 'row', 'col'), parts along dimension 0
The draws below stay inside these ranges and needn't reach their ends.
There are 2 independent parts, one for each index of `groups`. The reference program is written for one: setup_inputs(seed, part) draws one part's arguments, and reference() takes and returns one part's arrays. A program takes and returns all parts, laid end to end along the dimension named above; each array names one. Nothing has to cross between parts.
Inputs may be any that keep to these rules, and one draw needn't show every extreme that they name: `bin_index`: bin numbers may repeat. `block_order`: each of the 4 channel blocks once.
All inputs are finite; a program needn't handle non-finite values. No bound on the sum of `live_mask` on one device may be relied on, other than what follows from the above.
Results may differ from the reference program's by a relative error of at most 0.0059.
Values may be sent and summed in bfloat16 or wider, within the bound.
A program may use at most 192 MiB of HBM per device.

```python
import math
import jax
import jax.numpy as jnp
from jax import lax

C = 5120
S = 3072
W = 8
F = 4
RB = 1280
ROWB = 4


def draw_records(key, part):
    key = jax.random.fold_in(key, 11)
    noise_key, sample_key, channel_key = jax.random.split(key, 3)
    noise = jnp.clip(jax.random.normal(noise_key, (W, S, C), jnp.float32), -4.0, 4.0)
    ramp_top = 1.75
    channel_span = math.log(10.0)
    sample_scale = jnp.exp(jax.random.uniform(sample_key, (W, S, 1), jnp.float32) * math.log(10.0))
    ramp = 1.0 + (ramp_top - 1.0) * jnp.arange(S, dtype=jnp.float32) / S
    channel_scale = jnp.exp(jax.random.uniform(channel_key, (1, 1, C), jnp.float32) * channel_span)
    values = noise * sample_scale * ramp[None, :, None] * channel_scale
    return values.astype(jnp.bfloat16)


def touch_ends(entries, rng, low, largest):
    longest = entries.shape.index(max(entries.shape))
    spots = []
    for shift in (0, 1):
        where = [jax.random.randint(jax.random.fold_in(rng, axis), (), 0, length) for axis, length in enumerate(entries.shape)]
        where[longest] = (where[longest] + shift) % entries.shape[longest]
        spots.append(tuple(where))
    return entries.at[spots[0]].set(low).at[spots[1]].set(largest)


def setup_inputs(seed: int = 0, part: int = 0) -> dict:
    splits = jax.random.split(jax.random.key(seed), 5)
    part_keys = jax.random.split(jax.random.fold_in(splits[4], part), 5)
    records = draw_records(jax.random.fold_in(jax.random.fold_in(splits[4], part), 71), part)
    live_mask = touch_ends((jax.random.randint(part_keys[1], (C,), 0, 10) < 9).astype(jnp.int32), jax.random.fold_in(part_keys[1], 1), 0, 1)
    bin_index = touch_ends(jax.random.randint(part_keys[2], (F,), 1 + S // 512, S // 5), jax.random.fold_in(part_keys[2], 1), 1 + S // 512, (S // 5) - 1).astype(jnp.int32)
    block_order = jax.random.permutation(part_keys[3], ROWB).astype(jnp.int32)
    return dict(records=records, live_mask=live_mask, bin_index=bin_index, block_order=block_order)


def dft_rows(bin_index, positions):
    length = S
    phase_step = bin_index[:, None] * positions[None, :] % length
    angles = 2.0 * math.pi / length * phase_step.astype(jnp.float32)
    window = 0.5 - 0.5 * jnp.cos(2.0 * math.pi / length * positions.astype(jnp.float32))
    factor = math.sqrt(16.0 / (3.0 * length)) * window
    real_part = factor[None, :] * jnp.cos(angles)
    imag_part = -factor[None, :] * jnp.sin(angles)
    return jnp.stack([real_part, imag_part], axis=1).astype(jnp.bfloat16)

def reference(records, live_mask, bin_index, block_order):
    windows = records.shape[0]
    positions = jnp.arange(S, dtype=jnp.int32)
    dft_table = dft_rows(bin_index, positions).reshape(2 * F, S)

    def one_window(window_data):
        spectra = jnp.dot(dft_table, window_data, preferred_element_type=jnp.float32)
        energy = lax.optimization_barrier(jnp.sum(jnp.square(window_data.astype(jnp.float32)), axis=0))
        return (spectra, energy)
    spectra, energy = lax.map(one_window, records)
    scaling = live_mask.astype(jnp.float32)[None, :] / jnp.sqrt(energy / S + 1e-06)
    coeffs = (spectra * scaling[:, None, :]).astype(jnp.bfloat16).reshape(windows, F, 2, C)
    channel = jnp.arange(C, dtype=jnp.int32)
    source = block_order[channel // RB] * RB + channel % RB
    row_coeffs = jnp.take(coeffs, source, axis=3)

    def one_bin(bin_number):
        row_side = row_coeffs[:, bin_number].astype(jnp.float32)
        col_side = coeffs[:, bin_number].astype(jnp.float32)
        turned = jnp.stack([row_side[:, 1], -row_side[:, 0]], axis=1)
        paired = jnp.stack([row_side, turned], axis=1)
        return jnp.einsum('wpti,wtj->pij', paired, col_side) / windows
    return lax.map(one_bin, jnp.arange(F, dtype=jnp.int32))
```

```python
import functools
import math

import jax
import jax.numpy as jnp
from jax import lax
from jax.experimental import pallas as pl
from jax.experimental.pallas import tpu as pltpu
from jax.sharding import PartitionSpec as P

C = 5120
S = 3072
AHEAD = 3
TILE_ROWS = 256
MESH = pl.DeviceIdType.MESH


def dft_rows(bin_index, positions):
    length = S
    phase_step = bin_index[:, None] * positions[None, :] % length
    angles = 2.0 * math.pi / length * phase_step.astype(jnp.float32)
    window = 0.5 - 0.5 * jnp.cos(2.0 * math.pi / length * positions.astype(jnp.float32))
    factor = math.sqrt(16.0 / (3.0 * length)) * window
    real_part = factor[None, :] * jnp.cos(angles)
    imag_part = -factor[None, :] * jnp.sin(angles)
    return jnp.stack([real_part, imag_part], axis=1).astype(jnp.bfloat16)


def plain(records, live_mask, bin_index, block_order):
    half_windows, local_samples, channels = records.shape
    segment = lax.axis_index(("row", "col"))
    positions = segment * local_samples + jnp.arange(local_samples, dtype=jnp.int32)
    dft_table = dft_rows(bin_index, positions).reshape(-1, local_samples)
    spectra = jnp.einsum("ks,wsc->wkc", dft_table, records, preferred_element_type=jnp.float32)
    energy = jnp.sum(jnp.square(records.astype(jnp.float32)), axis=1, keepdims=True)
    block_width = live_mask.shape[0]
    spectra, energy = lax.psum((spectra, energy), ("row", "col"))
    offset = lax.axis_index("col") * block_width
    spectra = lax.dynamic_slice_in_dim(spectra, offset, block_width, 2)
    energy = lax.dynamic_slice_in_dim(energy, offset, block_width, 2)
    part_width = live_mask.shape[0]
    scaling = live_mask.astype(jnp.float32)[None, None, :] / jnp.sqrt(energy / S + 1e-06)
    total_bins = spectra.shape[1] // 2
    coeffs = (
        (spectra * scaling).astype(jnp.bfloat16).reshape(half_windows, total_bins, 2, part_width)
    )
    columns = lax.all_to_all(coeffs, "freq", split_axis=1, concat_axis=0, tiled=True)
    windows = columns.shape[0]
    row_width = C // lax.axis_size("row")
    per_block = block_width // row_width
    chosen = block_order[lax.axis_index("row")]
    own_slice = lax.dynamic_slice_in_dim(columns, chosen % per_block * row_width, row_width, 3)
    gathered = lax.all_gather(own_slice, "col", axis=3, tiled=True)
    sources = lax.dynamic_slice_in_dim(gathered, chosen // per_block * row_width, row_width, 3)
    turned = jnp.stack([sources[:, :, 1], -sources[:, :, 0]], axis=2)
    paired = jnp.stack([sources, turned], axis=1)
    products = jnp.einsum("wpbti,wbtj->bpij", paired, columns, preferred_element_type=jnp.float32)
    return products / windows


def coeffs_kernel(
    rows, width, table_ref, mask_ref, records_ref, out_ref,
    rec, part, xs, xr, zs, zr, ag,
    rec_sem, xs_sem, xr_sem, zs_sem, zr_sem, own_sem, gs_sem, gr_sem, fs_sem, fr_sem,
):
    r, c, f = lax.axis_index("row"), lax.axis_index("col"), lax.axis_index("freq")
    windows, samples = records_ref.shape[0], records_ref.shape[1]
    steps = 2 * rows

    def peer(step):
        return lax.rem(r + 1 + step, rows)

    def load(step):
        col = lax.rem(c + 1 + lax.div(step, rows), 2)
        start = pl.multiple_of((col * rows + peer(step)) * width, 128)
        return pltpu.make_async_copy(
            records_ref.at[:, :, pl.ds(start, width)], rec.at[step], rec_sem.at[step]
        )

    def x_copy(step):
        return pltpu.make_async_remote_copy(
            src_ref=xs.at[step], dst_ref=xr.at[step],
            send_sem=xs_sem.at[step], recv_sem=xr_sem.at[step],
            device_id={"col": 1 - c}, device_id_type=MESH,
        )

    def z_copy(step):
        return pltpu.make_async_remote_copy(
            src_ref=zs.at[step], dst_ref=zr.at[step],
            send_sem=zs_sem.at[step], recv_sem=zr_sem.at[step],
            device_id={"row": peer(step)}, device_id_type=MESH,
        )

    def piece(col, row, half):
        return out_ref.at[
            col,
            pl.ds(pl.multiple_of(half * 16, 16), 16),
            pl.ds(pl.multiple_of(row * width, 128), width),
        ]

    def compute(step):
        load(step).wait()
        for w in range(windows):
            part[8 * w : 8 * w + 8, :] = jnp.dot(
                table_ref[...], rec[step, w], preferred_element_type=jnp.float32
            )
            total = jnp.zeros((8, width), jnp.float32)
            for s in range(0, samples, 16):
                x = rec[step, w, s : s + 16, :].astype(jnp.float32)
                x = x * x
                total = total + (x[:8] + x[8:])
            part[32 + w : 33 + w, :] = jnp.sum(total, axis=0, keepdims=True)

    barrier = pltpu.get_barrier_semaphore()
    for step in range(rows - 1):
        for half in range(2):
            pl.semaphore_signal(
                barrier, inc=1, device_id={"row": peer(step), "freq": half}, device_id_type=MESH
            )
    pl.semaphore_signal(barrier, inc=1, device_id={"freq": 1 - f}, device_id_type=MESH)
    pl.semaphore_signal(barrier, inc=1, device_id={"col": 1 - c}, device_id_type=MESH)

    for step in range(AHEAD):
        load(step).start()
    part[...] = jnp.zeros_like(part)
    pl.semaphore_wait(barrier, 2 * rows)

    @pl.loop(0, rows)
    def _(step):
        load(step + AHEAD).start()
        compute(step)
        xs[step] = part[...].astype(xs.dtype)
        x_copy(step).start()

    @pl.loop(0, rows - 1)
    def _(step):
        @pl.when(step + rows + AHEAD < steps)
        def _():
            load(step + rows + AHEAD).start()

        compute(step + rows)
        x_copy(step).wait_recv()
        both = part[...] + xr[step].astype(jnp.float32)
        zs[step] = both[:40].astype(zs.dtype)
        z_copy(step).start()

    compute(steps - 1)
    x_copy(rows - 1).wait_recv()
    total = (part[...] + xr[rows - 1].astype(jnp.float32))[:40]
    for step in range(rows - 1):
        z_copy(step).wait_recv()
        total = total + zr[step].astype(jnp.float32)

    mask = mask_ref[:, pl.ds(pl.multiple_of(r * width, 128), width)].astype(jnp.float32)
    scaling = mask / jnp.sqrt(total[32:36] / S + 1e-06)
    coeffs = jnp.concatenate(
        [total[8 * w : 8 * w + 8] * scaling[w : w + 1] for w in range(windows)], axis=0
    ).astype(jnp.bfloat16)
    to = lax.broadcasted_iota(jnp.int32, (16, 32), 0)
    of = lax.broadcasted_iota(jnp.int32, (16, 32), 1)
    for half in range(2):
        pick = (of == (to // 4) * 8 + 4 * half + to % 4).astype(jnp.float32).astype(jnp.bfloat16)
        ag[half] = jnp.dot(pick, coeffs, preferred_element_type=jnp.float32).astype(jnp.bfloat16)

    def gather_copy(step, half, src_half):
        return pltpu.make_async_remote_copy(
            src_ref=ag.at[half], dst_ref=piece(c, r, f),
            send_sem=gs_sem.at[step, half], recv_sem=gr_sem.at[step, f],
            device_id={"row": peer(step), "freq": half}, device_id_type=MESH,
        )

    def arrival(step, half):
        row = lax.rem(r + rows - 1 - step, rows)
        return pltpu.make_async_remote_copy(
            src_ref=ag.at[0], dst_ref=piece(c, row, half),
            send_sem=gs_sem.at[step, half], recv_sem=gr_sem.at[step, half],
            device_id={"row": peer(step), "freq": half}, device_id_type=MESH,
        )

    def forward(step, half, src):
        row = lax.rem(r + rows - 1 - step, rows)
        return pltpu.make_async_remote_copy(
            src_ref=src, dst_ref=piece(c, row, half),
            send_sem=fs_sem.at[step, half], recv_sem=fr_sem.at[step, half],
            device_id={"col": 1 - c}, device_id_type=MESH,
        )

    def forwarded(step, half):
        row = lax.rem(r + rows - 1 - step, rows)
        return pltpu.make_async_remote_copy(
            src_ref=ag.at[0], dst_ref=piece(1 - c, row, half),
            send_sem=fs_sem.at[step, half], recv_sem=fr_sem.at[step, half],
            device_id={"col": 1 - c}, device_id_type=MESH,
        )

    last = rows - 1
    own = pltpu.make_async_copy(ag.at[f], piece(c, r, f), own_sem)
    own.start()
    to_core = pltpu.make_async_remote_copy(
        src_ref=ag.at[1 - f], dst_ref=piece(c, r, f),
        send_sem=gs_sem.at[last, 1 - f], recv_sem=gr_sem.at[last, f],
        device_id={"freq": 1 - f}, device_id_type=MESH,
    )
    for step in range(rows - 1):
        for half in range(2):
            gather_copy(step, half, half).start()
    to_core.start()
    forward(last, f, ag.at[f]).start()
    from_core = pltpu.make_async_remote_copy(
        src_ref=ag.at[0], dst_ref=piece(c, r, 1 - f),
        send_sem=gs_sem.at[last, f], recv_sem=gr_sem.at[last, 1 - f],
        device_id={"freq": 1 - f}, device_id_type=MESH,
    )
    from_core.wait_recv()
    forward(last, 1 - f, piece(c, r, 1 - f)).start()
    for step in range(rows - 1):
        for half in range(2):
            arrival(step, half).wait_recv()
            row = lax.rem(r + rows - 1 - step, rows)
            forward(step, half, piece(c, row, half)).start()

    for step in range(rows):
        for half in range(2):
            forwarded(step, half).wait_recv()
    own.wait()
    to_core.wait_send()
    for step in range(rows):
        x_copy(step).wait_send()
        for half in range(2):
            forwarded(step, half).wait_send()
    for step in range(rows - 1):
        z_copy(step).wait_send()
        for half in range(2):
            gather_copy(step, half, half).wait_send()


def products_kernel(row_width, scale, order_ref, coeffs_ref, out_ref):
    variant, tile = pl.program_id(0), pl.program_id(1)
    chosen = order_ref[lax.axis_index("row")]
    per_block = coeffs_ref.shape[2] // row_width
    tile_rows = out_ref.shape[2]
    start = pl.multiple_of(lax.rem(chosen, per_block) * row_width + tile * tile_rows, 128)
    sources = coeffs_ref[lax.div(chosen, per_block), :, pl.ds(start, tile_rows)]
    depth = sources.shape[0]
    of = lax.broadcasted_iota(jnp.int32, (depth, depth), 0)
    to = lax.broadcasted_iota(jnp.int32, (depth, depth), 1)
    imag = lax.rem(variant, 2)
    odd = to & 1
    same_bin = ((to >> 1) & 1) == lax.div(variant, 2)
    partner = to + imag * (1 - 2 * odd)
    sign = (1 - 2 * odd * imag).astype(jnp.float32)
    pick = jnp.where(same_bin & (of == partner), sign, 0.0).astype(jnp.bfloat16)
    paired = lax.dot_general(
        sources, pick, (((0,), (0,)), ((), ())), preferred_element_type=jnp.float32
    ).astype(jnp.bfloat16)
    columns = coeffs_ref[lax.axis_index("col")]
    out_ref[0, 0] = jnp.dot(paired, columns, preferred_element_type=jnp.float32) * scale


def local(records, live_mask, bin_index, block_order):
    half_windows, local_samples, channels = records.shape
    rows = lax.axis_size("row")
    block_width = live_mask.shape[0]
    width = block_width // rows
    row_width = C // rows
    segment = lax.axis_index(("row", "col"))
    positions = segment * local_samples + jnp.arange(local_samples, dtype=jnp.int32)
    table = dft_rows(bin_index, positions).reshape(-1, local_samples)
    vmem = pl.BlockSpec(memory_space=pltpu.VMEM)
    anywhere = pl.BlockSpec(memory_space=pl.ANY)
    dma = pltpu.SemaphoreType.DMA
    coeffs = pl.pallas_call(
        functools.partial(coeffs_kernel, rows, width),
        out_shape=jax.ShapeDtypeStruct((2, 32, block_width), jnp.bfloat16),
        in_specs=[vmem, vmem, anywhere],
        out_specs=anywhere,
        scratch_shapes=[
            pltpu.VMEM((2 * rows, half_windows, local_samples, width), jnp.bfloat16),
            pltpu.VMEM((48, width), jnp.float32),
            pltpu.VMEM((rows, 48, width), jnp.bfloat16),
            pltpu.VMEM((rows, 48, width), jnp.bfloat16),
            pltpu.VMEM((rows - 1, 40, width), jnp.float32),
            pltpu.VMEM((rows - 1, 40, width), jnp.float32),
            pltpu.VMEM((2, 16, width), jnp.bfloat16),
            dma((2 * rows,)),
            dma((rows,)),
            dma((rows,)),
            dma((rows - 1,)),
            dma((rows - 1,)),
            dma(()),
            dma((rows, 2)),
            dma((rows, 2)),
            dma((rows, 2)),
            dma((rows, 2)),
        ],
        compiler_params=pltpu.CompilerParams(
            collective_id=0, has_side_effects=True, vmem_limit_bytes=40 * 1024 * 1024
        ),
        cost_estimate=pl.CostEstimate(
            flops=18 * records.size, bytes_accessed=2 * records.size, transcendentals=0
        ),
        name="window_coeffs",
    )(table, live_mask.reshape(1, -1), records)
    out_shape = (2, 2, row_width, block_width)
    return pl.pallas_call(
        functools.partial(products_kernel, row_width, 1.0 / (2 * half_windows)),
        out_shape=jax.ShapeDtypeStruct(out_shape, jnp.float32),
        grid_spec=pltpu.PrefetchScalarGridSpec(
            num_scalar_prefetch=1,
            grid=(4, row_width // TILE_ROWS),
            in_specs=[pl.BlockSpec((2, 32, block_width), lambda v, i, order: (0, 0, 0))],
            out_specs=pl.BlockSpec(
                (1, 1, TILE_ROWS, block_width), lambda v, i, order: (v // 2, v % 2, i, 0)
            ),
        ),
        compiler_params=pltpu.CompilerParams(vmem_limit_bytes=32 * 1024 * 1024),
        cost_estimate=pl.CostEstimate(
            flops=64 * math.prod(out_shape),
            bytes_accessed=4 * math.prod(out_shape),
            transcendentals=0,
        ),
        name="cross_products",
    )(block_order, coeffs)


def solution(mesh):
    rows, cols = mesh.shape["row"], mesh.shape["col"]
    small = cols == 2 and mesh.shape["freq"] == 2 and rows == 4
    return jax.shard_map(
        local if small else plain,
        mesh=mesh,
        in_specs=(
            P(("groups", "freq"), ("row", "col"), None),
            P(("groups", "col")),
            P("groups"),
            P("groups"),
        ),
        out_specs=P(("groups", "freq"), None, "row", "col"),
        check_vma=False,
    )
```

```python
import functools
import math

import jax
import jax.numpy as jnp
from jax import lax
from jax.experimental import pallas as pl
from jax.experimental.pallas import tpu as pltpu
from jax.sharding import PartitionSpec as P

C = 5120
S = 3072
AHEAD = 3
TILE_ROWS = 256
SLOTS = 4
MESH = pl.DeviceIdType.MESH


def dft_rows(bin_index, positions):
    length = S
    phase_step = bin_index[:, None] * positions[None, :] % length
    angles = 2.0 * math.pi / length * phase_step.astype(jnp.float32)
    window = 0.5 - 0.5 * jnp.cos(2.0 * math.pi / length * positions.astype(jnp.float32))
    factor = math.sqrt(16.0 / (3.0 * length)) * window
    real_part = factor[None, :] * jnp.cos(angles)
    imag_part = -factor[None, :] * jnp.sin(angles)
    return jnp.stack([real_part, imag_part], axis=1).astype(jnp.bfloat16)


def plain(records, live_mask, bin_index, block_order):
    half_windows, local_samples, channels = records.shape
    segment = lax.axis_index(("row", "col"))
    positions = segment * local_samples + jnp.arange(local_samples, dtype=jnp.int32)
    dft_table = dft_rows(bin_index, positions).reshape(-1, local_samples)
    spectra = jnp.einsum("ks,wsc->wkc", dft_table, records, preferred_element_type=jnp.float32)
    energy = jnp.sum(jnp.square(records.astype(jnp.float32)), axis=1, keepdims=True)
    block_width = live_mask.shape[0]
    spectra, energy = lax.psum((spectra, energy), ("row", "col"))
    offset = lax.axis_index("col") * block_width
    spectra = lax.dynamic_slice_in_dim(spectra, offset, block_width, 2)
    energy = lax.dynamic_slice_in_dim(energy, offset, block_width, 2)
    part_width = live_mask.shape[0]
    scaling = live_mask.astype(jnp.float32)[None, None, :] / jnp.sqrt(energy / S + 1e-06)
    total_bins = spectra.shape[1] // 2
    coeffs = (
        (spectra * scaling).astype(jnp.bfloat16).reshape(half_windows, total_bins, 2, part_width)
    )
    columns = lax.all_to_all(coeffs, "freq", split_axis=1, concat_axis=0, tiled=True)
    windows = columns.shape[0]
    row_width = C // lax.axis_size("row")
    per_block = block_width // row_width
    chosen = block_order[lax.axis_index("row")]
    own_slice = lax.dynamic_slice_in_dim(columns, chosen % per_block * row_width, row_width, 3)
    gathered = lax.all_gather(own_slice, "col", axis=3, tiled=True)
    sources = lax.dynamic_slice_in_dim(gathered, chosen // per_block * row_width, row_width, 3)
    turned = jnp.stack([sources[:, :, 1], -sources[:, :, 0]], axis=2)
    paired = jnp.stack([sources, turned], axis=1)
    products = jnp.einsum("wpbti,wbtj->bpij", paired, columns, preferred_element_type=jnp.float32)
    return products / windows


def cosine(step):
    half, quarter = S // 2, S // 4
    fold = jnp.abs(step - half)
    angle = (2.0 * math.pi / S) * jnp.minimum(fold, half - fold).astype(jnp.float32)
    z = angle * angle
    value = jnp.full_like(z, 1.0 / math.factorial(16))
    for n in range(14, -1, -2):
        value = (-1.0) ** (n // 2) / math.factorial(n) + z * value
    return jnp.where(fold > quarter, value, -value)


def coeffs_kernel(
    rows, width, bins_ref, mask_ref, records_ref, out_ref,
    rec, table, part, xs, xr, zs, zr, ag,
    rec_sem, xs_sem, xr_sem, zs_sem, zr_sem, own_sem, gs_sem, gr_sem, fs_sem, fr_sem,
):
    r, c, f = lax.axis_index("row"), lax.axis_index("col"), lax.axis_index("freq")
    windows, samples = records_ref.shape[0], records_ref.shape[1]
    steps = 2 * rows

    def peer(step):
        return lax.rem(r + 1 + step, rows)

    def load(step):
        col = lax.rem(c + 1 + lax.div(step, rows), 2)
        start = pl.multiple_of((col * rows + peer(step)) * width, 128)
        return pltpu.make_async_copy(
            records_ref.at[:, :, pl.ds(start, width)], rec.at[step], rec_sem.at[step]
        )

    def x_copy(step):
        return pltpu.make_async_remote_copy(
            src_ref=xs.at[step], dst_ref=xr.at[step],
            send_sem=xs_sem.at[step], recv_sem=xr_sem.at[step],
            device_id={"col": 1 - c}, device_id_type=MESH,
        )

    def z_copy(step):
        return pltpu.make_async_remote_copy(
            src_ref=zs.at[step], dst_ref=zr.at[step],
            send_sem=zs_sem.at[step], recv_sem=zr_sem.at[step],
            device_id={"row": peer(step)}, device_id_type=MESH,
        )

    def piece(col, row, half):
        return out_ref.at[
            col,
            pl.ds(pl.multiple_of(half * 16, 16), 16),
            pl.ds(pl.multiple_of(row * width, 128), width),
        ]

    def compute(step):
        load(step).wait()
        for w in range(windows):
            part[8 * w : 8 * w + 8, :] = jnp.dot(
                table[...], rec[step, w], preferred_element_type=jnp.float32
            )
            total = jnp.zeros((8, width), jnp.float32)
            for s in range(0, samples, 16):
                x = rec[step, w, s : s + 16, :].astype(jnp.float32)
                x = x * x
                total = total + (x[:8] + x[8:])
            part[32 + w : 33 + w, :] = jnp.sum(total, axis=0, keepdims=True)

    barrier = pltpu.get_barrier_semaphore()
    for step in range(rows - 1):
        for half in range(2):
            pl.semaphore_signal(
                barrier, inc=1, device_id={"row": peer(step), "freq": half}, device_id_type=MESH
            )
    pl.semaphore_signal(barrier, inc=1, device_id={"freq": 1 - f}, device_id_type=MESH)
    pl.semaphore_signal(barrier, inc=1, device_id={"col": 1 - c}, device_id_type=MESH)

    for step in range(AHEAD):
        load(step).start()
    part[...] = jnp.zeros_like(part)
    row = lax.broadcasted_iota(jnp.int32, (8, samples), 0)
    position = (r * 2 + c) * samples + lax.broadcasted_iota(jnp.int32, (8, samples), 1)
    bins = jnp.zeros_like(row)
    for k in range(bins_ref.shape[0]):
        bins = jnp.where((row >> 1) == k, bins_ref[k], bins)
    phase = lax.rem(bins * position + (row & 1) * (S // 4), S)
    taper = math.sqrt(16.0 / (3.0 * S)) * (0.5 - 0.5 * cosine(position))
    table[...] = (taper * cosine(phase)).astype(table.dtype)
    pl.semaphore_wait(barrier, 2 * rows)

    @pl.loop(0, rows)
    def _(step):
        load(step + AHEAD).start()
        compute(step)
        xs[step] = part[...].astype(xs.dtype)
        x_copy(step).start()

    @pl.loop(0, rows - 1)
    def _(step):
        @pl.when(step + rows + AHEAD < steps)
        def _():
            load(step + rows + AHEAD).start()

        compute(step + rows)
        x_copy(step).wait_recv()
        both = part[...] + xr[step].astype(jnp.float32)
        zs[step] = both.astype(zs.dtype)
        z_copy(step).start()

    compute(steps - 1)
    x_copy(rows - 1).wait_recv()
    total = (part[...] + xr[rows - 1].astype(jnp.float32))[:40]
    for step in range(rows - 1):
        z_copy(step).wait_recv()
        total = total + zr[step].astype(jnp.float32)[:40]

    mask = mask_ref[pl.ds(pl.multiple_of(r * width, 128), width)].astype(jnp.float32)[None, :]
    scaling = mask / jnp.sqrt(total[32:36] / S + 1e-06)
    coeffs = jnp.concatenate(
        [total[8 * w : 8 * w + 8] * scaling[w : w + 1] for w in range(windows)], axis=0
    ).astype(jnp.bfloat16)
    to = lax.broadcasted_iota(jnp.int32, (16, 32), 0)
    of = lax.broadcasted_iota(jnp.int32, (16, 32), 1)
    for half in range(2):
        pick = (of == (to // 4) * 8 + 4 * half + to % 4).astype(jnp.float32).astype(jnp.bfloat16)
        ag[half] = jnp.dot(pick, coeffs, preferred_element_type=jnp.float32).astype(jnp.bfloat16)

    def gather_copy(step, half, src_half):
        return pltpu.make_async_remote_copy(
            src_ref=ag.at[half], dst_ref=piece(c, r, f),
            send_sem=gs_sem.at[step, half], recv_sem=gr_sem.at[step, f],
            device_id={"row": peer(step), "freq": half}, device_id_type=MESH,
        )

    def arrival(step, half):
        row = lax.rem(r + rows - 1 - step, rows)
        return pltpu.make_async_remote_copy(
            src_ref=ag.at[0], dst_ref=piece(c, row, half),
            send_sem=gs_sem.at[step, half], recv_sem=gr_sem.at[step, half],
            device_id={"row": peer(step), "freq": half}, device_id_type=MESH,
        )

    def forward(step, half, src):
        row = lax.rem(r + rows - 1 - step, rows)
        return pltpu.make_async_remote_copy(
            src_ref=src, dst_ref=piece(c, row, half),
            send_sem=fs_sem.at[step, half], recv_sem=fr_sem.at[step, half],
            device_id={"col": 1 - c}, device_id_type=MESH,
        )

    def forwarded(step, half):
        row = lax.rem(r + rows - 1 - step, rows)
        return pltpu.make_async_remote_copy(
            src_ref=ag.at[0], dst_ref=piece(1 - c, row, half),
            send_sem=fs_sem.at[step, half], recv_sem=fr_sem.at[step, half],
            device_id={"col": 1 - c}, device_id_type=MESH,
        )

    last = rows - 1
    own = pltpu.make_async_copy(ag.at[f], piece(c, r, f), own_sem)
    own.start()
    to_core = pltpu.make_async_remote_copy(
        src_ref=ag.at[1 - f], dst_ref=piece(c, r, f),
        send_sem=gs_sem.at[last, 1 - f], recv_sem=gr_sem.at[last, f],
        device_id={"freq": 1 - f}, device_id_type=MESH,
    )
    for step in range(rows - 1):
        for half in range(2):
            gather_copy(step, half, half).start()
    to_core.start()
    forward(last, f, ag.at[f]).start()
    from_core = pltpu.make_async_remote_copy(
        src_ref=ag.at[0], dst_ref=piece(c, r, 1 - f),
        send_sem=gs_sem.at[last, f], recv_sem=gr_sem.at[last, 1 - f],
        device_id={"freq": 1 - f}, device_id_type=MESH,
    )
    from_core.wait_recv()
    forward(last, 1 - f, piece(c, r, 1 - f)).start()
    for step in range(rows - 1):
        for half in range(2):
            arrival(step, half).wait_recv()
            row = lax.rem(r + rows - 1 - step, rows)
            forward(step, half, piece(c, row, half)).start()

    for step in range(rows):
        for half in range(2):
            forwarded(step, half).wait_recv()
    own.wait()
    to_core.wait_send()
    for step in range(rows):
        x_copy(step).wait_send()
        for half in range(2):
            forwarded(step, half).wait_send()
    for step in range(rows - 1):
        z_copy(step).wait_send()
        for half in range(2):
            gather_copy(step, half, half).wait_send()


def products_kernel(row_width, scale, order_ref, coeffs_ref, out_ref, ring, sem):
    slots, tile_rows = ring.shape[:2]
    tiles = row_width // tile_rows
    steps = 4 * tiles
    chosen = order_ref[lax.axis_index("row")]
    per_block = coeffs_ref.shape[2] // row_width
    first = lax.rem(chosen, per_block) * row_width

    def store(step):
        variant = lax.div(step, tiles)
        start = pl.multiple_of(lax.rem(step, tiles) * tile_rows, tile_rows)
        slot = lax.rem(step, slots)
        return pltpu.make_async_copy(
            ring.at[slot],
            out_ref.at[lax.div(variant, 2), lax.rem(variant, 2), pl.ds(start, tile_rows)],
            sem.at[slot],
        )

    @pl.loop(0, steps)
    def _(step):
        @pl.when(step >= slots)
        def _():
            store(step - slots).wait()

        variant = lax.div(step, tiles)
        start = pl.multiple_of(first + lax.rem(step, tiles) * tile_rows, 128)
        sources = coeffs_ref[lax.div(chosen, per_block), :, pl.ds(start, tile_rows)]
        depth = sources.shape[0]
        of = lax.broadcasted_iota(jnp.int32, (depth, depth), 0)
        to = lax.broadcasted_iota(jnp.int32, (depth, depth), 1)
        imag = lax.rem(variant, 2)
        odd = to & 1
        same_bin = ((to >> 1) & 1) == lax.div(variant, 2)
        partner = to + imag * (1 - 2 * odd)
        sign = (1 - 2 * odd * imag).astype(jnp.float32)
        pick = jnp.where(same_bin & (of == partner), sign, 0.0).astype(jnp.bfloat16)
        paired = lax.dot_general(
            sources, pick, (((0,), (0,)), ((), ())), preferred_element_type=jnp.float32
        ).astype(jnp.bfloat16)
        columns = coeffs_ref[lax.axis_index("col")]
        ring[lax.rem(step, slots)] = (
            jnp.dot(paired, columns, preferred_element_type=jnp.float32) * scale
        )
        store(step).start()

    for step in range(steps - slots, steps):
        store(step).wait()


def local(records, live_mask, bin_index, block_order):
    half_windows, local_samples, channels = records.shape
    rows = lax.axis_size("row")
    block_width = live_mask.shape[0]
    width = block_width // rows
    row_width = C // rows
    smem = pl.BlockSpec(memory_space=pltpu.SMEM)
    vmem = pl.BlockSpec(memory_space=pltpu.VMEM)
    anywhere = pl.BlockSpec(memory_space=pl.ANY)
    dma = pltpu.SemaphoreType.DMA
    coeffs = pl.pallas_call(
        functools.partial(coeffs_kernel, rows, width),
        out_shape=jax.ShapeDtypeStruct((2, 32, block_width), jnp.bfloat16),
        in_specs=[smem, vmem, anywhere],
        out_specs=anywhere,
        scratch_shapes=[
            pltpu.VMEM((2 * rows, half_windows, local_samples, width), jnp.bfloat16),
            pltpu.VMEM((8, local_samples), jnp.bfloat16),
            pltpu.VMEM((48, width), jnp.float32),
            pltpu.VMEM((rows, 48, width), jnp.bfloat16),
            pltpu.VMEM((rows, 48, width), jnp.bfloat16),
            pltpu.VMEM((rows - 1, 48, width), jnp.bfloat16),
            pltpu.VMEM((rows - 1, 48, width), jnp.bfloat16),
            pltpu.VMEM((2, 16, width), jnp.bfloat16),
            dma((2 * rows,)),
            dma((rows,)),
            dma((rows,)),
            dma((rows - 1,)),
            dma((rows - 1,)),
            dma(()),
            dma((rows, 2)),
            dma((rows, 2)),
            dma((rows, 2)),
            dma((rows, 2)),
        ],
        compiler_params=pltpu.CompilerParams(
            collective_id=0, has_side_effects=True, vmem_limit_bytes=40 * 1024 * 1024
        ),
        cost_estimate=pl.CostEstimate(
            flops=18 * records.size, bytes_accessed=2 * records.size, transcendentals=0
        ),
        name="window_coeffs",
    )(bin_index, live_mask, records)
    out_shape = (2, 2, row_width, block_width)
    return pl.pallas_call(
        functools.partial(products_kernel, row_width, 1.0 / (2 * half_windows)),
        out_shape=jax.ShapeDtypeStruct(out_shape, jnp.float32),
        in_specs=[smem, vmem],
        out_specs=anywhere,
        scratch_shapes=[
            pltpu.VMEM((SLOTS, TILE_ROWS, block_width), jnp.float32),
            dma((SLOTS,)),
        ],
        compiler_params=pltpu.CompilerParams(vmem_limit_bytes=32 * 1024 * 1024),
        cost_estimate=pl.CostEstimate(
            flops=64 * math.prod(out_shape),
            bytes_accessed=4 * math.prod(out_shape),
            transcendentals=0,
        ),
        name="cross_products",
    )(block_order, coeffs)


def solution(mesh):
    rows, cols = mesh.shape["row"], mesh.shape["col"]
    small = cols == 2 and mesh.shape["freq"] == 2 and rows == 4
    return jax.shard_map(
        local if small else plain,
        mesh=mesh,
        in_specs=(
            P(("groups", "freq"), ("row", "col"), None),
            P(("groups", "col")),
            P("groups"),
            P("groups"),
        ),
        out_specs=P(("groups", "freq"), None, "row", "col"),
        check_vma=False,
    )
```

```python
import functools
import math

import jax
import jax.numpy as jnp
from jax import lax
from jax.experimental import pallas as pl
from jax.experimental.pallas import tpu as pltpu
from jax.sharding import PartitionSpec as P

C = 5120
S = 3072
TILE_ROWS = 256
SLOTS = 4
MESH = pl.DeviceIdType.MESH


def dft_rows(bin_index, positions):
    length = S
    phase_step = bin_index[:, None] * positions[None, :] % length
    angles = 2.0 * math.pi / length * phase_step.astype(jnp.float32)
    window = 0.5 - 0.5 * jnp.cos(2.0 * math.pi / length * positions.astype(jnp.float32))
    factor = math.sqrt(16.0 / (3.0 * length)) * window
    real_part = factor[None, :] * jnp.cos(angles)
    imag_part = -factor[None, :] * jnp.sin(angles)
    return jnp.stack([real_part, imag_part], axis=1).astype(jnp.bfloat16)


def plain(records, live_mask, bin_index, block_order):
    half_windows, local_samples, channels = records.shape
    segment = lax.axis_index(("row", "col"))
    positions = segment * local_samples + jnp.arange(local_samples, dtype=jnp.int32)
    dft_table = dft_rows(bin_index, positions).reshape(-1, local_samples)
    spectra = jnp.einsum("ks,wsc->wkc", dft_table, records, preferred_element_type=jnp.float32)
    energy = jnp.sum(jnp.square(records.astype(jnp.float32)), axis=1, keepdims=True)
    block_width = live_mask.shape[0]
    spectra, energy = lax.psum((spectra, energy), ("row", "col"))
    offset = lax.axis_index("col") * block_width
    spectra = lax.dynamic_slice_in_dim(spectra, offset, block_width, 2)
    energy = lax.dynamic_slice_in_dim(energy, offset, block_width, 2)
    part_width = live_mask.shape[0]
    scaling = live_mask.astype(jnp.float32)[None, None, :] / jnp.sqrt(energy / S + 1e-06)
    total_bins = spectra.shape[1] // 2
    coeffs = (
        (spectra * scaling).astype(jnp.bfloat16).reshape(half_windows, total_bins, 2, part_width)
    )
    columns = lax.all_to_all(coeffs, "freq", split_axis=1, concat_axis=0, tiled=True)
    windows = columns.shape[0]
    row_width = C // lax.axis_size("row")
    per_block = block_width // row_width
    chosen = block_order[lax.axis_index("row")]
    own_slice = lax.dynamic_slice_in_dim(columns, chosen % per_block * row_width, row_width, 3)
    gathered = lax.all_gather(own_slice, "col", axis=3, tiled=True)
    sources = lax.dynamic_slice_in_dim(gathered, chosen // per_block * row_width, row_width, 3)
    turned = jnp.stack([sources[:, :, 1], -sources[:, :, 0]], axis=2)
    paired = jnp.stack([sources, turned], axis=1)
    products = jnp.einsum("wpbti,wbtj->bpij", paired, columns, preferred_element_type=jnp.float32)
    return products / windows


def cosine(step):
    half, quarter = S // 2, S // 4
    fold = jnp.abs(step - half)
    angle = (2.0 * math.pi / S) * jnp.minimum(fold, half - fold).astype(jnp.float32)
    z = angle * angle
    value = jnp.full_like(z, 1.0 / math.factorial(16))
    for n in range(14, -1, -2):
        value = (-1.0) ** (n // 2) / math.factorial(n) + z * value
    return jnp.where(fold > quarter, value, -value)


def coeffs_kernel(
    rows, width, bins_ref, mask_ref, records_ref, out_ref,
    rec, bins, mask, table, part, xs, xr, zs, zr, ag,
    rec_sem, bins_sem, mask_sem, xs_sem, xr_sem, zs_sem, zr_sem, own_sem, gs_sem, gr_sem, fs_sem, fr_sem,
):
    r, c, f = lax.axis_index("row"), lax.axis_index("col"), lax.axis_index("freq")
    windows, samples = records_ref.shape[0], records_ref.shape[1]
    steps = 2 * rows

    def peer(step):
        return lax.rem(r + 1 + step, rows)

    def load(step):
        col = lax.rem(c + 1 + lax.div(step, rows), 2)
        start = pl.multiple_of((col * rows + peer(step)) * width, 128)
        return pltpu.make_async_copy(
            records_ref.at[:, :, pl.ds(start, width)], rec.at[step], rec_sem.at[step]
        )

    def x_copy(step):
        return pltpu.make_async_remote_copy(
            src_ref=xs.at[step], dst_ref=xr.at[step],
            send_sem=xs_sem.at[step], recv_sem=xr_sem.at[step],
            device_id={"col": 1 - c}, device_id_type=MESH,
        )

    def z_copy(step):
        return pltpu.make_async_remote_copy(
            src_ref=zs.at[step], dst_ref=zr.at[step],
            send_sem=zs_sem.at[step], recv_sem=zr_sem.at[step],
            device_id={"row": peer(step)}, device_id_type=MESH,
        )

    def piece(col, row, half):
        return out_ref.at[
            col,
            pl.ds(pl.multiple_of(half * 16, 16), 16),
            pl.ds(pl.multiple_of(row * width, 128), width),
        ]

    def compute(step):
        load(step).wait()
        for w in range(windows):
            part[8 * w : 8 * w + 8, :] = jnp.dot(
                table[...], rec[step, w], preferred_element_type=jnp.float32
            )
            total = jnp.zeros((8, width), jnp.float32)
            for s in range(0, samples, 16):
                x = rec[step, w, s : s + 16, :].astype(jnp.float32)
                x = x * x
                total = total + (x[:8] + x[8:])
            part[32 + w : 33 + w, :] = jnp.sum(total, axis=0, keepdims=True)

    barrier = pltpu.get_barrier_semaphore()
    for step in range(rows - 1):
        for half in range(2):
            pl.semaphore_signal(
                barrier, inc=1, device_id={"row": peer(step), "freq": half}, device_id_type=MESH
            )
    pl.semaphore_signal(barrier, inc=1, device_id={"freq": 1 - f}, device_id_type=MESH)
    pl.semaphore_signal(barrier, inc=1, device_id={"col": 1 - c}, device_id_type=MESH)

    bins_copy = pltpu.make_async_copy(bins_ref, bins, bins_sem)
    bins_copy.start()
    mask_copy = pltpu.make_async_copy(mask_ref, mask, mask_sem)
    mask_copy.start()
    for step in (0, 1, rows):
        load(step).start()
    part[...] = jnp.zeros_like(part)
    row = lax.broadcasted_iota(jnp.int32, (8, samples), 0)
    position = (r * 2 + c) * samples + lax.broadcasted_iota(jnp.int32, (8, samples), 1)
    bins_copy.wait()
    bin_rows = jnp.zeros_like(row)
    for k in range(bins.shape[0]):
        bin_rows = jnp.where((row >> 1) == k, bins[k], bin_rows)
    phase = lax.rem(bin_rows * position + (row & 1) * (S // 4), S)
    taper = math.sqrt(16.0 / (3.0 * S)) * (0.5 - 0.5 * cosine(position))
    table[...] = (taper * cosine(phase)).astype(table.dtype)
    pl.semaphore_wait(barrier, 2 * rows)

    def send_x(step):
        compute(step)
        xs[step] = part[...].astype(xs.dtype)
        x_copy(step).start()

    send_x(0)

    @pl.loop(0, rows - 1)
    def _(step):
        @pl.when(step + 2 < rows)
        def _():
            load(step + 2).start()

        load(rows + step + 1).start()
        send_x(step + 1)
        compute(step + rows)
        x_copy(step).wait_recv()
        both = part[...] + xr[step].astype(jnp.float32)
        zs[step] = both.astype(zs.dtype)
        z_copy(step).start()

    compute(steps - 1)
    x_copy(rows - 1).wait_recv()
    total = (part[...] + xr[rows - 1].astype(jnp.float32))[:40]
    for step in range(rows - 1):
        z_copy(step).wait_recv()
        total = total + zr[step].astype(jnp.float32)[:40]

    mask_copy.wait()
    live = mask[pl.ds(pl.multiple_of(r * width, 128), width)].astype(jnp.float32)[None, :]
    scaling = live / jnp.sqrt(total[32:36] / S + 1e-06)
    coeffs = jnp.concatenate(
        [total[8 * w : 8 * w + 8] * scaling[w : w + 1] for w in range(windows)], axis=0
    ).astype(jnp.bfloat16)
    to = lax.broadcasted_iota(jnp.int32, (16, 32), 0)
    of = lax.broadcasted_iota(jnp.int32, (16, 32), 1)
    for half in range(2):
        pick = (of == (to // 4) * 8 + 4 * half + to % 4).astype(jnp.float32).astype(jnp.bfloat16)
        ag[half] = jnp.dot(pick, coeffs, preferred_element_type=jnp.float32).astype(jnp.bfloat16)

    def gather_copy(step, half, src_half):
        return pltpu.make_async_remote_copy(
            src_ref=ag.at[half], dst_ref=piece(c, r, f),
            send_sem=gs_sem.at[step, half], recv_sem=gr_sem.at[step, f],
            device_id={"row": peer(step), "freq": half}, device_id_type=MESH,
        )

    def arrival(step, half):
        row = lax.rem(r + rows - 1 - step, rows)
        return pltpu.make_async_remote_copy(
            src_ref=ag.at[0], dst_ref=piece(c, row, half),
            send_sem=gs_sem.at[step, half], recv_sem=gr_sem.at[step, half],
            device_id={"row": peer(step), "freq": half}, device_id_type=MESH,
        )

    def forward(step, half, src):
        row = lax.rem(r + rows - 1 - step, rows)
        return pltpu.make_async_remote_copy(
            src_ref=src, dst_ref=piece(c, row, half),
            send_sem=fs_sem.at[step, half], recv_sem=fr_sem.at[step, half],
            device_id={"col": 1 - c}, device_id_type=MESH,
        )

    def forwarded(step, half):
        row = lax.rem(r + rows - 1 - step, rows)
        return pltpu.make_async_remote_copy(
            src_ref=ag.at[0], dst_ref=piece(1 - c, row, half),
            send_sem=fs_sem.at[step, half], recv_sem=fr_sem.at[step, half],
            device_id={"col": 1 - c}, device_id_type=MESH,
        )

    last = rows - 1
    own = pltpu.make_async_copy(ag.at[f], piece(c, r, f), own_sem)
    own.start()
    to_core = pltpu.make_async_remote_copy(
        src_ref=ag.at[1 - f], dst_ref=piece(c, r, f),
        send_sem=gs_sem.at[last, 1 - f], recv_sem=gr_sem.at[last, f],
        device_id={"freq": 1 - f}, device_id_type=MESH,
    )
    for step in range(rows - 1):
        for half in range(2):
            gather_copy(step, half, half).start()
    to_core.start()
    forward(last, f, ag.at[f]).start()
    from_core = pltpu.make_async_remote_copy(
        src_ref=ag.at[0], dst_ref=piece(c, r, 1 - f),
        send_sem=gs_sem.at[last, f], recv_sem=gr_sem.at[last, 1 - f],
        device_id={"freq": 1 - f}, device_id_type=MESH,
    )
    from_core.wait_recv()
    forward(last, 1 - f, piece(c, r, 1 - f)).start()
    for step in range(rows - 1):
        for half in range(2):
            arrival(step, half).wait_recv()
            row = lax.rem(r + rows - 1 - step, rows)
            forward(step, half, piece(c, row, half)).start()

    for step in range(rows):
        for half in range(2):
            forwarded(step, half).wait_recv()
    own.wait()
    to_core.wait_send()
    for step in range(rows):
        x_copy(step).wait_send()
        for half in range(2):
            forwarded(step, half).wait_send()
    for step in range(rows - 1):
        z_copy(step).wait_send()
        for half in range(2):
            gather_copy(step, half, half).wait_send()


def products_kernel(row_width, scale, order_ref, coeffs_ref, out_ref, ring, sem):
    slots, tile_rows = ring.shape[:2]
    tiles = row_width // tile_rows
    steps = 4 * tiles
    chosen = order_ref[lax.axis_index("row")]
    per_block = coeffs_ref.shape[2] // row_width
    first = lax.rem(chosen, per_block) * row_width

    def store(step):
        variant = lax.div(step, tiles)
        start = pl.multiple_of(lax.rem(step, tiles) * tile_rows, tile_rows)
        slot = lax.rem(step, slots)
        return pltpu.make_async_copy(
            ring.at[slot],
            out_ref.at[lax.div(variant, 2), lax.rem(variant, 2), pl.ds(start, tile_rows)],
            sem.at[slot],
        )

    @pl.loop(0, steps)
    def _(step):
        @pl.when(step >= slots)
        def _():
            store(step - slots).wait()

        variant = lax.div(step, tiles)
        start = pl.multiple_of(first + lax.rem(step, tiles) * tile_rows, 128)
        sources = coeffs_ref[lax.div(chosen, per_block), :, pl.ds(start, tile_rows)]
        depth = sources.shape[0]
        of = lax.broadcasted_iota(jnp.int32, (depth, depth), 0)
        to = lax.broadcasted_iota(jnp.int32, (depth, depth), 1)
        imag = lax.rem(variant, 2)
        odd = to & 1
        same_bin = ((to >> 1) & 1) == lax.div(variant, 2)
        partner = to + imag * (1 - 2 * odd)
        sign = (1 - 2 * odd * imag).astype(jnp.float32)
        pick = jnp.where(same_bin & (of == partner), sign, 0.0).astype(jnp.bfloat16)
        paired = lax.dot_general(
            sources, pick, (((0,), (0,)), ((), ())), preferred_element_type=jnp.float32
        ).astype(jnp.bfloat16)
        columns = coeffs_ref[lax.axis_index("col")]
        ring[lax.rem(step, slots)] = (
            jnp.dot(paired, columns, preferred_element_type=jnp.float32) * scale
        )
        store(step).start()

    for step in range(steps - slots, steps):
        store(step).wait()


def local(records, live_mask, bin_index, block_order):
    half_windows, local_samples, channels = records.shape
    rows = lax.axis_size("row")
    block_width = live_mask.shape[0]
    width = block_width // rows
    row_width = C // rows
    smem = pl.BlockSpec(memory_space=pltpu.SMEM)
    hbm = pl.BlockSpec(memory_space=pltpu.HBM)
    vmem = pl.BlockSpec(memory_space=pltpu.VMEM)
    anywhere = pl.BlockSpec(memory_space=pl.ANY)
    dma = pltpu.SemaphoreType.DMA
    coeffs = pl.pallas_call(
        functools.partial(coeffs_kernel, rows, width),
        out_shape=jax.ShapeDtypeStruct((2, 32, block_width), jnp.bfloat16),
        in_specs=[hbm, hbm, anywhere],
        out_specs=anywhere,
        scratch_shapes=[
            pltpu.VMEM((2 * rows, half_windows, local_samples, width), jnp.bfloat16),
            pltpu.SMEM(bin_index.shape, jnp.int32),
            pltpu.VMEM((block_width,), jnp.int32),
            pltpu.VMEM((8, local_samples), jnp.bfloat16),
            pltpu.VMEM((48, width), jnp.float32),
            pltpu.VMEM((rows, 48, width), jnp.bfloat16),
            pltpu.VMEM((rows, 48, width), jnp.bfloat16),
            pltpu.VMEM((rows - 1, 48, width), jnp.bfloat16),
            pltpu.VMEM((rows - 1, 48, width), jnp.bfloat16),
            pltpu.VMEM((2, 16, width), jnp.bfloat16),
            dma((2 * rows,)),
            dma(()),
            dma(()),
            dma((rows,)),
            dma((rows,)),
            dma((rows - 1,)),
            dma((rows - 1,)),
            dma(()),
            dma((rows, 2)),
            dma((rows, 2)),
            dma((rows, 2)),
            dma((rows, 2)),
        ],
        compiler_params=pltpu.CompilerParams(
            collective_id=0, has_side_effects=True, vmem_limit_bytes=40 * 1024 * 1024
        ),
        cost_estimate=pl.CostEstimate(
            flops=18 * records.size, bytes_accessed=2 * records.size, transcendentals=0
        ),
        name="window_coeffs",
    )(bin_index, live_mask, records)
    out_shape = (2, 2, row_width, block_width)
    return pl.pallas_call(
        functools.partial(products_kernel, row_width, 1.0 / (2 * half_windows)),
        out_shape=jax.ShapeDtypeStruct(out_shape, jnp.float32),
        in_specs=[smem, vmem],
        out_specs=anywhere,
        scratch_shapes=[
            pltpu.VMEM((SLOTS, TILE_ROWS, block_width), jnp.float32),
            dma((SLOTS,)),
        ],
        compiler_params=pltpu.CompilerParams(vmem_limit_bytes=32 * 1024 * 1024),
        cost_estimate=pl.CostEstimate(
            flops=64 * math.prod(out_shape),
            bytes_accessed=4 * math.prod(out_shape),
            transcendentals=0,
        ),
        name="cross_products",
    )(block_order, coeffs)


def solution(mesh):
    rows, cols = mesh.shape["row"], mesh.shape["col"]
    small = cols == 2 and mesh.shape["freq"] == 2 and rows == 4
    return jax.shard_map(
        local if small else plain,
        mesh=mesh,
        in_specs=(
            P(("groups", "freq"), ("row", "col"), None),
            P(("groups", "col")),
            P("groups"),
            P("groups"),
        ),
        out_specs=P(("groups", "freq"), None, "row", "col"),
        check_vma=False,
    )
```

```python
import functools
import math

import jax
import jax.numpy as jnp
from jax import lax
from jax.experimental import pallas as pl
from jax.experimental.pallas import tpu as pltpu
from jax.sharding import PartitionSpec as P

C = 5120
S = 3072
AHEAD = 3
TILE_ROWS = 256
SLOTS = 4
MESH = pl.DeviceIdType.MESH


def dft_rows(bin_index, positions):
    length = S
    phase_step = bin_index[:, None] * positions[None, :] % length
    angles = 2.0 * math.pi / length * phase_step.astype(jnp.float32)
    window = 0.5 - 0.5 * jnp.cos(2.0 * math.pi / length * positions.astype(jnp.float32))
    factor = math.sqrt(16.0 / (3.0 * length)) * window
    real_part = factor[None, :] * jnp.cos(angles)
    imag_part = -factor[None, :] * jnp.sin(angles)
    return jnp.stack([real_part, imag_part], axis=1).astype(jnp.bfloat16)


def plain(records, live_mask, bin_index, block_order):
    half_windows, local_samples, channels = records.shape
    segment = lax.axis_index(("row", "col"))
    positions = segment * local_samples + jnp.arange(local_samples, dtype=jnp.int32)
    dft_table = dft_rows(bin_index, positions).reshape(-1, local_samples)
    spectra = jnp.einsum("ks,wsc->wkc", dft_table, records, preferred_element_type=jnp.float32)
    energy = jnp.sum(jnp.square(records.astype(jnp.float32)), axis=1, keepdims=True)
    block_width = live_mask.shape[0]
    spectra, energy = lax.psum((spectra, energy), ("row", "col"))
    offset = lax.axis_index("col") * block_width
    spectra = lax.dynamic_slice_in_dim(spectra, offset, block_width, 2)
    energy = lax.dynamic_slice_in_dim(energy, offset, block_width, 2)
    part_width = live_mask.shape[0]
    scaling = live_mask.astype(jnp.float32)[None, None, :] / jnp.sqrt(energy / S + 1e-06)
    total_bins = spectra.shape[1] // 2
    coeffs = (
        (spectra * scaling).astype(jnp.bfloat16).reshape(half_windows, total_bins, 2, part_width)
    )
    columns = lax.all_to_all(coeffs, "freq", split_axis=1, concat_axis=0, tiled=True)
    windows = columns.shape[0]
    row_width = C // lax.axis_size("row")
    per_block = block_width // row_width
    chosen = block_order[lax.axis_index("row")]
    own_slice = lax.dynamic_slice_in_dim(columns, chosen % per_block * row_width, row_width, 3)
    gathered = lax.all_gather(own_slice, "col", axis=3, tiled=True)
    sources = lax.dynamic_slice_in_dim(gathered, chosen // per_block * row_width, row_width, 3)
    turned = jnp.stack([sources[:, :, 1], -sources[:, :, 0]], axis=2)
    paired = jnp.stack([sources, turned], axis=1)
    products = jnp.einsum("wpbti,wbtj->bpij", paired, columns, preferred_element_type=jnp.float32)
    return products / windows


def cosine(step):
    half, quarter = S // 2, S // 4
    fold = jnp.abs(step - half)
    angle = (2.0 * math.pi / S) * jnp.minimum(fold, half - fold).astype(jnp.float32)
    z = angle * angle
    value = jnp.full_like(z, 1.0 / math.factorial(16))
    for n in range(14, -1, -2):
        value = (-1.0) ** (n // 2) / math.factorial(n) + z * value
    return jnp.where(fold > quarter, value, -value)


def coeffs_kernel(
    rows, width, bins_ref, mask_ref, records_ref, out_ref,
    rec, bins, mask, table, part, xs, xr, zs, zr, ag,
    rec_sem, bins_sem, mask_sem, xs_sem, xr_sem, zs_sem, zr_sem, own_sem, gs_sem, gr_sem, fs_sem, fr_sem,
):
    r, c, f = lax.axis_index("row"), lax.axis_index("col"), lax.axis_index("freq")
    windows, samples = records_ref.shape[0], records_ref.shape[1]
    steps = 2 * rows

    def peer(step):
        return lax.rem(r + 1 + step, rows)

    def load(step):
        col = lax.rem(c + 1 + lax.div(step, rows), 2)
        start = pl.multiple_of((col * rows + peer(step)) * width, 128)
        return pltpu.make_async_copy(
            records_ref.at[:, :, pl.ds(start, width)], rec.at[step], rec_sem.at[step]
        )

    def x_copy(step):
        return pltpu.make_async_remote_copy(
            src_ref=xs.at[step], dst_ref=xr.at[step],
            send_sem=xs_sem.at[step], recv_sem=xr_sem.at[step],
            device_id={"col": 1 - c}, device_id_type=MESH,
        )

    def z_copy(step):
        return pltpu.make_async_remote_copy(
            src_ref=zs.at[step], dst_ref=zr.at[step],
            send_sem=zs_sem.at[step], recv_sem=zr_sem.at[step],
            device_id={"row": peer(step)}, device_id_type=MESH,
        )

    def piece(col, row, half):
        return out_ref.at[
            col,
            pl.ds(pl.multiple_of(half * 16, 16), 16),
            pl.ds(pl.multiple_of(row * width, 128), width),
        ]

    def compute(step):
        load(step).wait()
        for w in range(windows):
            part[8 * w : 8 * w + 8, :] = jnp.dot(
                table[...], rec[step, w], preferred_element_type=jnp.float32
            )
            total = jnp.zeros((8, width), jnp.float32)
            for s in range(0, samples, 16):
                x = rec[step, w, s : s + 16, :].astype(jnp.float32)
                x = x * x
                total = total + (x[:8] + x[8:])
            part[32 + w : 33 + w, :] = jnp.sum(total, axis=0, keepdims=True)

    barrier = pltpu.get_barrier_semaphore()
    for step in range(rows - 1):
        for half in range(2):
            pl.semaphore_signal(
                barrier, inc=1, device_id={"row": peer(step), "freq": half}, device_id_type=MESH
            )
    pl.semaphore_signal(barrier, inc=1, device_id={"freq": 1 - f}, device_id_type=MESH)
    pl.semaphore_signal(barrier, inc=1, device_id={"col": 1 - c}, device_id_type=MESH)

    bins_copy = pltpu.make_async_copy(bins_ref, bins, bins_sem)
    bins_copy.start()
    mask_copy = pltpu.make_async_copy(mask_ref, mask, mask_sem)
    mask_copy.start()
    for step in range(AHEAD):
        load(step).start()
    part[...] = jnp.zeros_like(part)
    row = lax.broadcasted_iota(jnp.int32, (8, samples), 0)
    position = (r * 2 + c) * samples + lax.broadcasted_iota(jnp.int32, (8, samples), 1)
    bins_copy.wait()
    bin_rows = jnp.zeros_like(row)
    for k in range(bins.shape[0]):
        bin_rows = jnp.where((row >> 1) == k, bins[k], bin_rows)
    phase = lax.rem(bin_rows * position + (row & 1) * (S // 4), S)
    taper = math.sqrt(16.0 / (3.0 * S)) * (0.5 - 0.5 * cosine(position))
    table[...] = (taper * cosine(phase)).astype(table.dtype)
    pl.semaphore_wait(barrier, 2 * rows)

    @pl.loop(0, rows)
    def _(step):
        load(step + AHEAD).start()
        compute(step)
        xs[step] = part[...].astype(xs.dtype)
        x_copy(step).start()

    @pl.loop(0, rows - 1)
    def _(step):
        @pl.when(step + rows + AHEAD < steps)
        def _():
            load(step + rows + AHEAD).start()

        compute(step + rows)
        x_copy(step).wait_recv()
        both = part[...] + xr[step].astype(jnp.float32)
        zs[step] = both.astype(zs.dtype)
        z_copy(step).start()

    compute(steps - 1)
    x_copy(rows - 1).wait_recv()
    total = (part[...] + xr[rows - 1].astype(jnp.float32))[:40]
    for step in range(rows - 1):
        z_copy(step).wait_recv()
        total = total + zr[step].astype(jnp.float32)[:40]

    mask_copy.wait()
    live = mask[pl.ds(pl.multiple_of(r * width, 128), width)].astype(jnp.float32)[None, :]
    scaling = live / jnp.sqrt(total[32:36] / S + 1e-06)
    coeffs = jnp.concatenate(
        [total[8 * w : 8 * w + 8] * scaling[w : w + 1] for w in range(windows)], axis=0
    ).astype(jnp.bfloat16)
    to = lax.broadcasted_iota(jnp.int32, (16, 32), 0)
    of = lax.broadcasted_iota(jnp.int32, (16, 32), 1)
    for half in range(2):
        pick = (of == (to // 4) * 8 + 4 * half + to % 4).astype(jnp.float32).astype(jnp.bfloat16)
        ag[half] = jnp.dot(pick, coeffs, preferred_element_type=jnp.float32).astype(jnp.bfloat16)

    def gather_copy(step, half, src_half):
        return pltpu.make_async_remote_copy(
            src_ref=ag.at[half], dst_ref=piece(c, r, f),
            send_sem=gs_sem.at[step, half], recv_sem=gr_sem.at[step, f],
            device_id={"row": peer(step), "freq": half}, device_id_type=MESH,
        )

    def arrival(step, half):
        row = lax.rem(r + rows - 1 - step, rows)
        return pltpu.make_async_remote_copy(
            src_ref=ag.at[0], dst_ref=piece(c, row, half),
            send_sem=gs_sem.at[step, half], recv_sem=gr_sem.at[step, half],
            device_id={"row": peer(step), "freq": half}, device_id_type=MESH,
        )

    def forward(step, half, src):
        row = lax.rem(r + rows - 1 - step, rows)
        return pltpu.make_async_remote_copy(
            src_ref=src, dst_ref=piece(c, row, half),
            send_sem=fs_sem.at[step, half], recv_sem=fr_sem.at[step, half],
            device_id={"col": 1 - c}, device_id_type=MESH,
        )

    def forwarded(step, half):
        row = lax.rem(r + rows - 1 - step, rows)
        return pltpu.make_async_remote_copy(
            src_ref=ag.at[0], dst_ref=piece(1 - c, row, half),
            send_sem=fs_sem.at[step, half], recv_sem=fr_sem.at[step, half],
            device_id={"col": 1 - c}, device_id_type=MESH,
        )

    last = rows - 1
    own = pltpu.make_async_copy(ag.at[f], piece(c, r, f), own_sem)
    own.start()
    to_core = pltpu.make_async_remote_copy(
        src_ref=ag.at[1 - f], dst_ref=piece(c, r, f),
        send_sem=gs_sem.at[last, 1 - f], recv_sem=gr_sem.at[last, f],
        device_id={"freq": 1 - f}, device_id_type=MESH,
    )
    for step in range(rows - 1):
        for half in range(2):
            gather_copy(step, half, half).start()
    to_core.start()
    forward(last, f, ag.at[f]).start()
    from_core = pltpu.make_async_remote_copy(
        src_ref=ag.at[0], dst_ref=piece(c, r, 1 - f),
        send_sem=gs_sem.at[last, f], recv_sem=gr_sem.at[last, 1 - f],
        device_id={"freq": 1 - f}, device_id_type=MESH,
    )
    from_core.wait_recv()
    forward(last, 1 - f, piece(c, r, 1 - f)).start()
    for step in range(rows - 1):
        for half in range(2):
            arrival(step, half).wait_recv()
            row = lax.rem(r + rows - 1 - step, rows)
            forward(step, half, piece(c, row, half)).start()

    for step in range(rows):
        for half in range(2):
            forwarded(step, half).wait_recv()
    own.wait()
    to_core.wait_send()
    for step in range(rows):
        x_copy(step).wait_send()
        for half in range(2):
            forwarded(step, half).wait_send()
    for step in range(rows - 1):
        z_copy(step).wait_send()
        for half in range(2):
            gather_copy(step, half, half).wait_send()


def products_kernel(row_width, scale, order_ref, coeffs_ref, out_ref, ring, sem):
    slots, tile_rows = ring.shape[:2]
    tiles = row_width // tile_rows
    steps = 4 * tiles
    chosen = order_ref[lax.axis_index("row")]
    per_block = coeffs_ref.shape[2] // row_width
    first = lax.rem(chosen, per_block) * row_width

    def store(step):
        variant = lax.div(step, tiles)
        start = pl.multiple_of(lax.rem(step, tiles) * tile_rows, tile_rows)
        slot = lax.rem(step, slots)
        return pltpu.make_async_copy(
            ring.at[slot],
            out_ref.at[lax.div(variant, 2), lax.rem(variant, 2), pl.ds(start, tile_rows)],
            sem.at[slot],
        )

    @pl.loop(0, steps)
    def _(step):
        @pl.when(step >= slots)
        def _():
            store(step - slots).wait()

        variant = lax.div(step, tiles)
        start = pl.multiple_of(first + lax.rem(step, tiles) * tile_rows, 128)
        sources = coeffs_ref[lax.div(chosen, per_block), :, pl.ds(start, tile_rows)]
        depth = sources.shape[0]
        of = lax.broadcasted_iota(jnp.int32, (depth, depth), 0)
        to = lax.broadcasted_iota(jnp.int32, (depth, depth), 1)
        imag = lax.rem(variant, 2)
        odd = to & 1
        same_bin = ((to >> 1) & 1) == lax.div(variant, 2)
        partner = to + imag * (1 - 2 * odd)
        sign = (1 - 2 * odd * imag).astype(jnp.float32)
        pick = jnp.where(same_bin & (of == partner), sign, 0.0).astype(jnp.bfloat16)
        paired = lax.dot_general(
            sources, pick, (((0,), (0,)), ((), ())), preferred_element_type=jnp.float32
        ).astype(jnp.bfloat16)
        columns = coeffs_ref[lax.axis_index("col")]
        ring[lax.rem(step, slots)] = (
            jnp.dot(paired, columns, preferred_element_type=jnp.float32) * scale
        )
        store(step).start()

    for step in range(steps - slots, steps):
        store(step).wait()


def local(records, live_mask, bin_index, block_order):
    half_windows, local_samples, channels = records.shape
    rows = lax.axis_size("row")
    block_width = live_mask.shape[0]
    width = block_width // rows
    row_width = C // rows
    smem = pl.BlockSpec(memory_space=pltpu.SMEM)
    hbm = pl.BlockSpec(memory_space=pltpu.HBM)
    vmem = pl.BlockSpec(memory_space=pltpu.VMEM)
    anywhere = pl.BlockSpec(memory_space=pl.ANY)
    dma = pltpu.SemaphoreType.DMA
    coeffs = pl.pallas_call(
        functools.partial(coeffs_kernel, rows, width),
        out_shape=jax.ShapeDtypeStruct((2, 32, block_width), jnp.bfloat16),
        in_specs=[hbm, hbm, anywhere],
        out_specs=anywhere,
        scratch_shapes=[
            pltpu.VMEM((2 * rows, half_windows, local_samples, width), jnp.bfloat16),
            pltpu.SMEM(bin_index.shape, jnp.int32),
            pltpu.VMEM((block_width,), jnp.int32),
            pltpu.VMEM((8, local_samples), jnp.bfloat16),
            pltpu.VMEM((48, width), jnp.float32),
            pltpu.VMEM((rows, 48, width), jnp.bfloat16),
            pltpu.VMEM((rows, 48, width), jnp.bfloat16),
            pltpu.VMEM((rows - 1, 48, width), jnp.bfloat16),
            pltpu.VMEM((rows - 1, 48, width), jnp.bfloat16),
            pltpu.VMEM((2, 16, width), jnp.bfloat16),
            dma((2 * rows,)),
            dma(()),
            dma(()),
            dma((rows,)),
            dma((rows,)),
            dma((rows - 1,)),
            dma((rows - 1,)),
            dma(()),
            dma((rows, 2)),
            dma((rows, 2)),
            dma((rows, 2)),
            dma((rows, 2)),
        ],
        compiler_params=pltpu.CompilerParams(
            collective_id=0, has_side_effects=True, vmem_limit_bytes=65152 * 1024
        ),
        cost_estimate=pl.CostEstimate(
            flops=18 * records.size, bytes_accessed=2 * records.size, transcendentals=0
        ),
        name="window_coeffs",
    )(bin_index, live_mask, records)
    out_shape = (2, 2, row_width, block_width)
    return pl.pallas_call(
        functools.partial(products_kernel, row_width, 1.0 / (2 * half_windows)),
        out_shape=jax.ShapeDtypeStruct(out_shape, jnp.float32),
        in_specs=[smem, vmem],
        out_specs=anywhere,
        scratch_shapes=[
            pltpu.VMEM((SLOTS, TILE_ROWS, block_width), jnp.float32),
            dma((SLOTS,)),
        ],
        compiler_params=pltpu.CompilerParams(vmem_limit_bytes=65152 * 1024),
        cost_estimate=pl.CostEstimate(
            flops=64 * math.prod(out_shape),
            bytes_accessed=4 * math.prod(out_shape),
            transcendentals=0,
        ),
        name="cross_products",
    )(block_order, coeffs)


def solution(mesh):
    rows, cols = mesh.shape["row"], mesh.shape["col"]
    small = cols == 2 and mesh.shape["freq"] == 2 and rows == 4
    return jax.shard_map(
        local if small else plain,
        mesh=mesh,
        in_specs=(
            P(("groups", "freq"), ("row", "col"), None),
            P(("groups", "col")),
            P("groups"),
            P("groups"),
        ),
        out_specs=P(("groups", "freq"), None, "row", "col"),
        check_vma=False,
    )
```
